512 devices in a mesh: gx: 32 (over x, y, z_hi), gy: 16 (over z_lo, core).
Axes of the slice: x: 4, y: 4, z: 16 (z_hi: 2, z_lo: 8; z = z_hi * 8 + z_lo), core: 2. Of those that a mesh axis runs over, the one named last changes fastest.
Arguments:
- sea_level: float32 [4096, 12288], P('gy', 'gx'), may hold values from -6 to 6
- transport_u: float32 [4096, 12288], P('gy', 'gx'), may hold values from -6 to 6
- transport_v: float32 [4096, 12288], P('gy', 'gx'), may hold values from -6 to 6
- ocean_depth: float32 [4096, 12288], P('gy', 'gx'), may hold values from 0.5 to 2
- tracers: float32 [2, 4096, 12288], P(None, 'gy', 'gx'), may hold values from -6 to 6
- land_mask: int32 [4096, 12288], P('gy', 'gx'), may hold values 0 or 1
Outputs:
- new_level: float32 [4096, 12288], P('gy', 'gx')
- new_east_flow: float32 [4096, 12288], P('gy', 'gx')
- new_north_flow: float32 [4096, 12288], P('gy', 'gx')
- new_tracers: float32 [2, 4096, 12288], P(None, 'gy', 'gx')
The draws below stay inside these ranges and needn't reach their ends.
All inputs are finite; a program needn't handle non-finite values. No bound on the sum of `land_mask` on one device may be relied on, other than what follows from the above.
Results may differ from the reference program's by a relative error of at most 0.00002.
Values sent between devices are 32-bit elements; how exact they have to be, the bound alone decides.
A program may use at most 64 MiB of HBM per device.

```python
import math
import jax
import jax.numpy as jnp

SUBSTEPS = 3
NX = 12288
NY = 4096


def set_ends(entries, stream_key, low, largest):
    dims = entries.shape
    index_at = [jax.random.randint(jax.random.fold_in(stream_key, axis), (), 0, dims[axis]) for axis in range(len(dims))]
    entries = entries.at[tuple(index_at)].set(low)
    longest = dims.index(max(dims))
    index_at[longest] = (index_at[longest] + 1) % dims[longest]
    return entries.at[tuple(index_at)].set(largest)


def level_of(stream_key, dims, pieces, least, largest):
    loudness = 1.0
    for axis_at, blocks in pieces:
        heights = jax.random.uniform(jax.random.fold_in(jax.random.fold_in(stream_key, 6), axis_at), (blocks,), jnp.float32, least / len(pieces), largest / len(pieces))
        loudness = loudness * jnp.repeat(jnp.exp(heights), dims[axis_at] // blocks).reshape((-1,) + (1,) * (len(dims) - 1 - axis_at))
    return loudness


def scatter_about(rng, extent, deviation, limit, pieces=(), held_as=jnp.bfloat16):
    array = jax.random.normal(rng, extent, jnp.float32) * deviation
    if len(pieces) > 0:
        array = level_of(rng, extent, pieces, -0.22, 0.18) * array
    return jnp.clip(array, min=-limit, max=limit).astype(held_as)


def setup_inputs(seed: int = 0) -> dict:
    arg_keys = jax.random.split(jax.random.key(seed), 7)
    sea_level = scatter_about(arg_keys[0], (NY, NX), 1.0, 6.0, ((0, 16), (1, 32)), jnp.float32)
    transport_u = scatter_about(arg_keys[1], (NY, NX), 1.0, 6.0, ((0, 16), (1, 32)), jnp.float32)
    transport_v = scatter_about(arg_keys[2], (NY, NX), 1.0, 6.0, ((0, 16), (1, 32)), jnp.float32)
    ocean_depth = jnp.clip(jnp.exp(math.log(2.0) - 1.3862944 * jax.random.uniform(arg_keys[3], (NY, NX), jnp.float32) ** level_of(arg_keys[3], (NY, NX), ((0, 16), (1, 32)), -0.2, 0.2)), 0.5, 2.0)
    tracers = scatter_about(arg_keys[4], (2, NY, NX), 1.0, 6.0, ((1, 16), (2, 32)), jnp.float32)
    land_mask = set_ends((jax.random.randint(arg_keys[5], (NY, NX), 0, 4) < 3).astype(jnp.int32), jax.random.fold_in(arg_keys[5], 1), 0, 1)
    return {"sea_level": sea_level, "transport_u": transport_u, "transport_v": transport_v, "ocean_depth": ocean_depth, "tracers": tracers, "land_mask": land_mask}


DIVERGENCE_STEP = 0.3
GRAVITY_STEP = 0.3
DRAG_RATE = 0.05
CORIOLIS_TOP = 0.4
ADVECT_STEP = 0.1


def mirror(field):
    return field[..., ::-1]


def west_of(field):
    return jnp.roll(field, 1, axis=-1)


def east_of(field):
    return jnp.roll(field, -1, axis=-1)


def south_of(field):
    return jnp.concatenate([jnp.zeros_like(field[..., :1, :]), field[..., :-1, :]], axis=-2)


def north_of(field, ghost):
    return jnp.concatenate([field[..., 1:, :], ghost[..., None, :]], axis=-2)


def fold_top(field):
    top_row = field[-1]
    return field.at[-1].set(0.5 * (top_row - mirror(top_row)))


def reference(sea_level, transport_u, transport_v, ocean_depth, tracers, land_mask):
    sea_mask = land_mask.astype(jnp.float32)
    east_mask = sea_mask * east_of(sea_mask)
    north_mask = sea_mask * north_of(sea_mask, mirror(sea_mask[-1]))
    depth_u = 0.5 * (ocean_depth + east_of(ocean_depth))
    depth_v = 0.5 * (ocean_depth + north_of(ocean_depth, mirror(ocean_depth[-1])))
    row_index = jnp.arange(NY).astype(jnp.float32)
    coriolis_u = (CORIOLIS_TOP * ((row_index + 0.5) / NY))[:, None]
    coriolis_v = (CORIOLIS_TOP * ((row_index + 1.0) / NY))[:, None]
    east_flow = east_mask * transport_u
    north_flow = north_mask * transport_v
    level = sea_level
    sum_east = jnp.zeros_like(east_flow)
    sum_north = jnp.zeros_like(north_flow)
    for substep in range(SUBSTEPS):
        flow_west = west_of(east_flow)
        pair_sum = flow_west + east_flow
        north_sym = fold_top(north_flow)
        sym_south = south_of(north_sym)
        level = level - DIVERGENCE_STEP * sea_mask * (east_flow - flow_west + north_sym - sym_south)
        mean_v = 0.25 * (north_sym + east_of(north_sym) + sym_south + east_of(sym_south))
        mean_u = 0.25 * (pair_sum + north_of(pair_sum, -mirror(pair_sum[-1])))
        level_above = north_of(level, mirror(level[-1]))
        new_east = east_mask * ((1.0 - DRAG_RATE / depth_u) * east_flow - GRAVITY_STEP * depth_u * (east_of(level) - level) + coriolis_u * mean_v)
        north_flow = north_mask * ((1.0 - DRAG_RATE / depth_v) * north_sym - GRAVITY_STEP * depth_v * (level_above - level) - coriolis_v * mean_u)
        east_flow = new_east
        sum_east = sum_east + east_flow
        sum_north = sum_north + north_flow
    mean_east = sum_east / SUBSTEPS
    mean_north = fold_top(sum_north / SUBSTEPS)
    tracer_east = east_of(tracers)
    tracer_above = north_of(tracers, mirror(tracers[:, -1]))
    flux_east = jnp.maximum(mean_east, 0.0) * tracers + jnp.minimum(mean_east, 0.0) * tracer_east
    flux_north = jnp.maximum(mean_north, 0.0) * tracers + jnp.minimum(mean_north, 0.0) * tracer_above
    change = flux_east - west_of(flux_east) + flux_north - south_of(flux_north)
    new_tracers = tracers - ADVECT_STEP * sea_mask * change / ocean_depth
    return (level, east_flow, north_flow, new_tracers)
```

```python
import functools

import jax
import jax.numpy as jnp
from jax import lax
from jax.experimental import pallas as pl
from jax.experimental.pallas import tpu as pltpu
from jax.sharding import PartitionSpec as P

SUBSTEPS = 3
DIVERGENCE_STEP = 0.3
GRAVITY_STEP = 0.3
DRAG_RATE = 0.05
CORIOLIS_TOP = 0.4
ADVECT_STEP = 0.1

MESH = pl.DeviceIdType.MESH
FIELDS = 7
U, V, LEVEL, MASK, DEPTH, T0, T1 = range(FIELDS)
GROUP = 16
BLOCK = 32
W, E, S, N, SW, SE, NW, NE = range(8)


def roll(x, shift, axis):
    return pltpu.roll(x, shift % x.shape[axis], axis)


def lanes(shape):
    return lax.broadcasted_iota(jnp.int32, shape, 1)


def sublanes(shape):
    return lax.broadcasted_iota(jnp.int32, shape, 0)


def advance(u, v, level, mask, depth, tracers, cor_u, cor_v, row_axis, fold=None):
    col_axis = 1 - row_axis
    west = lambda x: roll(x, 1, col_axis)
    east = lambda x: roll(x, -1, col_axis)
    south = lambda x: roll(x, 1, row_axis)
    north = lambda x: roll(x, -1, row_axis)
    head = lambda x: x[:8]

    def sym(x, other):
        return jnp.concatenate([jnp.where(fold[0], 0.5 * (head(x) - other), head(x)), x[8:]], axis=0)

    east_mask = mask * east(mask)
    north_mask = mask * north(mask)
    depth_u = 0.5 * (depth + east(depth))
    depth_v = 0.5 * (depth + north(depth))
    keep_u = east_mask * (1.0 - DRAG_RATE / depth_u)
    keep_v = north_mask * (1.0 - DRAG_RATE / depth_v)
    push_u = east_mask * (GRAVITY_STEP * depth_u)
    push_v = north_mask * (GRAVITY_STEP * depth_v)
    turn_u = east_mask * (0.25 * cor_u)
    turn_v = north_mask * (0.25 * cor_v)
    spread = DIVERGENCE_STEP * mask
    u = east_mask * u
    v = north_mask * v
    if fold is not None:
        other = head(north_mask) * fold[1]
    for step in range(SUBSTEPS):
        if fold is not None:
            v, other = sym(v, other), 0.5 * (other - head(v))
        flow_west = west(u)
        pair = flow_west + u
        sym_south = south(v)
        level = level - spread * (u - flow_west + v - sym_south)
        both = v + sym_south
        pairs = pair + north(pair)
        slope_v = north(level) - level
        new_u = keep_u * u - push_u * (east(level) - level) + turn_u * (both + east(both))
        if fold is not None:
            other = head(keep_v) * other + head(push_v) * head(slope_v) + head(turn_v) * head(pairs)
        v = keep_v * v - push_v * slope_v - turn_v * pairs
        u = new_u
        sum_u = u if step == 0 else sum_u + u
        sum_v = v if step == 0 else sum_v + v
        if fold is not None:
            sum_other = other if step == 0 else sum_other + other
    mean_u = sum_u * (1.0 / SUBSTEPS)
    mean_v = sum_v * (1.0 / SUBSTEPS)
    if fold is not None:
        mean_v = sym(mean_v, sum_other * (1.0 / SUBSTEPS))
    out_u, in_u = jnp.maximum(mean_u, 0.0), jnp.minimum(mean_u, 0.0)
    out_v, in_v = jnp.maximum(mean_v, 0.0), jnp.minimum(mean_v, 0.0)
    rate = ADVECT_STEP * mask / depth
    new = []
    for t in tracers:
        flux_u = out_u * t + in_u * east(t)
        flux_v = out_v * t + in_v * north(t)
        new.append(t - rate * (flux_u - west(flux_u) + flux_v - south(flux_v)))
    return level, u, v, new[0], new[1]


def pack_last(x):
    s = sublanes(x[0].shape)
    return [
        jnp.where(s < 4, roll(x[U], 4, 0), x[V]),
        jnp.where(s < 4, roll(x[LEVEL], 4, 0), x[MASK]),
        jnp.where(s < 4, roll(x[DEPTH], 4, 0), jnp.where(s < 6, roll(x[T0], 6, 0), x[T1])),
    ]


def pack_first(x):
    s = sublanes(x[0].shape)
    return [
        jnp.where(s < 4, x[U], roll(x[V], 4, 0)),
        jnp.where(s < 4, x[LEVEL], roll(x[MASK], 4, 0)),
        jnp.where(s < 4, x[DEPTH], jnp.where(s < 6, roll(x[T0], 4, 0), roll(x[T1], 6, 0))),
    ]


def unpack_last(ref):
    a, b, c = ref[0:8], ref[8:16], ref[16:24]
    return [roll(a, 4, 0), a, roll(b, 4, 0), b, roll(c, 4, 0), roll(c, 2, 0), c]


def unpack_first(ref):
    a, b, c = ref[0:8], ref[8:16], ref[16:24]
    return [a, roll(a, 4, 0), b, roll(b, 4, 0), c, roll(c, 4, 0), roll(c, 2, 0)]


def flip(x, axis, group):
    at = lax.broadcasted_iota(jnp.int32, x.shape, axis)
    bit = 1
    while bit < group:
        x = jnp.where(at & bit == 0, roll(x, -bit, axis), roll(x, bit, axis))
        bit *= 2
    return x


def exchange_kernel(
    level_in, u_in, v_in, depth_in, tracers_in, land_in,
    level_out, u_out, v_out, tracers_out,
    x, land, packed, packed_t, send_cols, send_rows, got_cols, got_rows, got_corners, halo_t, strip, other,
    load_sem, send_sem, recv_sem,
):
    rows, cols = u_out.shape
    nx, ny = lax.axis_size("gx"), lax.axis_size("gy")
    me_x, me_y = lax.axis_index("gx"), lax.axis_index("gy")
    to_e, to_w = lax.rem(me_x + 1, nx), lax.rem(me_x + nx - 1, nx)
    top, bottom = me_y == ny - 1, me_y == 0
    past = lambda column: jnp.where(top, nx - 1 - column, column)
    to_n, to_s = jnp.where(top, me_y, me_y + 1), jnp.where(bottom, me_y, me_y - 1)
    own_ne, own_nw = top & (past(to_e) == me_x), top & (past(to_w) == me_x)
    has_s = jnp.logical_not(bottom)

    barrier = pltpu.get_barrier_semaphore()

    def greet(to_x, to_y):
        pl.semaphore_signal(barrier, inc=1, device_id=(to_x, to_y), device_id_type=MESH)

    greet(to_w, me_y)
    greet(to_e, me_y)
    greet(past(me_x), to_n)
    pl.when(jnp.logical_not(own_ne))(lambda: greet(past(to_e), to_n))
    pl.when(jnp.logical_not(own_nw))(lambda: greet(past(to_w), to_n))

    @pl.when(has_s)
    def _():
        greet(me_x, to_s)
        greet(to_e, to_s)
        greet(to_w, to_s)

    inner = pl.ds(8, rows)
    loads = [
        pltpu.make_async_copy(land_in, land, load_sem.at[0]),
        pltpu.make_async_copy(u_in, x.at[U, inner], load_sem.at[1]),
        pltpu.make_async_copy(v_in, x.at[V, inner], load_sem.at[2]),
        pltpu.make_async_copy(level_in, x.at[LEVEL, inner], load_sem.at[3]),
        pltpu.make_async_copy(depth_in, x.at[DEPTH, inner], load_sem.at[4]),
        pltpu.make_async_copy(tracers_in, x.at[pl.ds(T0, 2), inner], load_sem.at[5]),
    ]
    for load in loads:
        load.start()
    for f in range(FIELDS):
        x[f, 0:8] = jnp.ones((8, cols), jnp.float32)
        x[f, rows + 8 : rows + 16] = jnp.ones((8, cols), jnp.float32)
    for load in loads:
        load.wait()

    size = 64

    def pack_columns(k, carry):
        at = pl.multiple_of(k * size, size)
        x[MASK, pl.ds(at + 8, size)] = land[pl.ds(at, size)].astype(jnp.float32)
        lane = lanes((size, 128))
        result = None
        for f in range(FIELDS):
            first = x[f, pl.ds(at + 8, size), 0:128]
            last = x[f, pl.ds(at + 8, size), cols - 128 : cols]
            ends = roll(jnp.where(lane < 64, first, last), f * GROUP + 8, 1)
            result = ends if f == 0 else jnp.where(lane < f * GROUP, result, ends)
        packed[pl.ds(at, size)] = result
        return carry

    lax.fori_loop(0, rows // size, pack_columns, 0, unroll=True)
    packed_t[...] = packed[...].T

    def put(ref, at, parts):
        for k, part in enumerate(parts):
            ref[at, 8 * k : 8 * k + 8] = part

    groups = [GROUP * f for f in range(FIELDS)]
    put(send_cols, 0, pack_last([packed_t[g : g + 8] for g in groups]))
    put(send_cols, 1, pack_first([packed_t[g + 8 : g + 16] for g in groups]))
    put(send_rows, 0, pack_last([x[f, rows : rows + 8] for f in range(FIELDS)]))
    put(send_rows, 1, pack_first([x[f, 8:16] for f in range(FIELDS)]))

    def copy(source, target, k, at, to_x, to_y):
        return pltpu.make_async_remote_copy(
            src_ref=source,
            dst_ref=target,
            send_sem=send_sem.at[k],
            recv_sem=recv_sem.at[at],
            device_id=(to_x, to_y),
            device_id_type=MESH,
        )

    north_rows, south_rows = packed.at[pl.ds(rows - 8, 8)], packed.at[pl.ds(0, 8)]
    corner = lambda at: got_corners.at[at - SW]
    away_e = copy(send_cols.at[0], got_cols.at[W], E, W, to_e, me_y)
    away_w = copy(send_cols.at[1], got_cols.at[E], W, E, to_w, me_y)
    away_s = copy(send_rows.at[1], got_rows.at[1], S, N, me_x, to_s)
    away_se = copy(south_rows, corner(NW), SE, NW, to_e, to_s)
    away_sw = copy(south_rows, corner(NE), SW, NE, to_w, to_s)
    away_n = copy(send_rows.at[0], got_rows.at[0], N, S, me_x, to_n)
    away_ne = copy(north_rows, corner(SW), NE, SW, to_e, to_n)
    away_nw = copy(north_rows, corner(SE), NW, SE, to_w, to_n)
    fold_n = copy(send_rows.at[0], got_rows.at[1], N, N, past(me_x), to_n)
    fold_ne = copy(north_rows, corner(NE), NE, NE, past(to_e), to_n)
    fold_nw = copy(north_rows, corner(NW), NW, NW, past(to_w), to_n)
    not_top = jnp.logical_not(top)
    far_ne, far_nw = top & jnp.logical_not(own_ne), top & jnp.logical_not(own_nw)

    count = 3 + jnp.where(own_ne, 0, 1) + jnp.where(own_nw, 0, 1) + jnp.where(has_s, 3, 0)
    pl.semaphore_wait(barrier, count)
    away_e.start()
    away_w.start()

    @pl.when(not_top)
    def _():
        away_ne.start()
        away_nw.start()
        away_n.start()

    @pl.when(top)
    def _():
        fold_n.start()

    pl.when(far_ne)(lambda: fold_ne.start())
    pl.when(far_nw)(lambda: fold_nw.start())

    @pl.when(has_s)
    def _():
        away_se.start()
        away_sw.start()
        away_s.start()

    def coriolis(row):
        row = row.astype(jnp.float32)
        total = 1.0 * ny * rows
        return CORIOLIS_TOP * ((row + 0.5) / total), CORIOLIS_TOP * ((row + 1.0) / total)

    def compute_inner(k, carry):
        at = pl.multiple_of(k * BLOCK, BLOCK)
        part = [x[f, pl.ds(at, BLOCK + 16)] for f in range(FIELDS)]
        row = me_y * rows + at - 8 + sublanes((BLOCK + 16, 1))
        out = advance(*part[:5], part[5:], *coriolis(row), 0)
        keep = pl.ds(at, BLOCK)
        level_out[keep] = out[0][8 : BLOCK + 8]
        u_out[keep] = out[1][8 : BLOCK + 8]
        v_out[keep] = out[2][8 : BLOCK + 8]
        tracers_out[0, keep] = out[3][8 : BLOCK + 8]
        tracers_out[1, keep] = out[4][8 : BLOCK + 8]
        return carry

    lax.fori_loop(0, rows // BLOCK, compute_inner, 0)

    away_w.wait_recv()
    away_e.wait_recv()
    away_s.wait_recv()

    @pl.when(has_s)
    def _():
        away_n.wait_recv()
        away_ne.wait_recv()
        away_nw.wait_recv()

    pl.when(jnp.logical_not(own_nw))(lambda: away_se.wait_recv())
    pl.when(jnp.logical_not(own_ne))(lambda: away_sw.wait_recv())

    @pl.when(own_nw)
    def _():
        corner(NW)[...] = north_rows[...]

    @pl.when(own_ne)
    def _():
        corner(NE)[...] = north_rows[...]

    from_w, from_e = unpack_last(got_cols.at[W]), unpack_first(got_cols.at[E])
    for f, g in enumerate(groups):
        halo_t[g : g + 8] = from_w[f]
        halo_t[g + 8 : g + 16] = from_e[f]
    halo_t[GROUP * FIELDS :] = jnp.ones((128 - GROUP * FIELDS, rows), jnp.float32)

    def put_rows(at, parts, sides):
        for f in range(FIELDS):
            strip[f, at : at + 8, 0:cols] = parts[f]
            strip[f, at : at + 8, cols : cols + 128] = roll(sides, -(GROUP * f + 8), 1)

    put_rows(0, [x[f, rows : rows + 8] for f in range(FIELDS)], halo_t[:, rows - 128 : rows].T[120:128])
    put_rows(24, [x[f, 8:16] for f in range(FIELDS)], halo_t[:, 0:128].T[0:8])
    eastern = lanes((8, 128)) & 8 != 0

    @pl.when(not_top)
    def _():
        put_rows(8, unpack_first(got_rows.at[1]), jnp.where(eastern, corner(NE)[...], corner(NW)[...]))
        other[...] = jnp.zeros_like(other)

    @pl.when(top)
    def _():
        parts = [flip(part, 0, 8) for part in unpack_last(got_rows.at[1])]
        tiles = range(0, cols, 128)
        parts = [
            jnp.concatenate([flip(part[:, c : c + 128], 1, 128) for c in reversed(tiles)], axis=1)
            for part in parts
        ]
        sides = jnp.where(eastern, corner(NW)[...], corner(NE)[...])
        put_rows(8, parts, flip(flip(sides, 0, 8), 1, GROUP))
        strip[U, 8:16] = -roll(strip[U, 8:16], -1, 1)
        mirrored = strip[V, 8:16]
        strip[V, 8:16] = -roll(mirrored, -1, 0)
        other[...] = roll(mirrored, -1, 0)

    @pl.when(has_s)
    def _():
        put_rows(16, unpack_last(got_rows.at[0]), jnp.where(eastern, corner(SE)[...], corner(SW)[...]))

    @pl.when(bottom)
    def _():
        for f in range(FIELDS):
            strip[f, 16:24] = jnp.full((8, cols + 128), 1.0 if f == DEPTH else 0.0, jnp.float32)

    parts = [
        jnp.concatenate([packed_t[g : g + 8], halo_t[g + 8 : g + 16], halo_t[g : g + 8], packed_t[g + 8 : g + 16]], axis=0)
        for g in groups
    ]
    row = me_y * rows + lanes((1, rows))
    by_col = advance(*parts[:5], parts[5:], *coriolis(row), 1)

    s = sublanes((32, 1))
    row = me_y * rows + jnp.where(s < 16, rows - 8 + s, s - 24)
    total = ny * rows
    cor_u = coriolis(jnp.where(row >= total, 2 * total - 1 - row, row))[0]
    cor_v = coriolis(jnp.where(row >= total, 2 * total - 2 - row, row))[1]
    parts = [strip[f] for f in range(FIELDS)]
    at_fold = top & (sublanes((8, cols + 128)) == 7)
    by_row = advance(*parts[:5], parts[5:], cor_u, cor_v, 0, (at_fold, other[...]))

    zeros = jnp.zeros((128 - GROUP * 5, rows), jnp.float32)
    back = jnp.concatenate([part for o in by_col for part in (o[0:8], o[24:32])] + [zeros], axis=0).T
    outs = [level_out, u_out, v_out, tracers_out.at[0], tracers_out.at[1]]
    lane = lanes((rows, 128))
    s = sublanes((8, cols))
    for o, out in enumerate(outs):
        ends = roll(back, -(GROUP * o + 8), 1)
        out[:, 0:128] = jnp.where(lane < 4, ends, out[:, 0:128])
        out[:, cols - 128 : cols] = jnp.where(lane >= 124, ends, out[:, cols - 128 : cols])
        out[0:8] = jnp.where(s < 4, by_row[o][24:32, 0:cols], out[0:8])
        out[rows - 8 : rows] = jnp.where(s >= 4, by_row[o][0:8, 0:cols], out[rows - 8 : rows])

    away_e.wait_send()
    away_w.wait_send()

    @pl.when(not_top)
    def _():
        away_ne.wait_send()
        away_nw.wait_send()
        away_n.wait_send()

    @pl.when(top)
    def _():
        fold_n.wait_send()

    pl.when(far_ne)(lambda: fold_ne.wait_send())
    pl.when(far_nw)(lambda: fold_nw.wait_send())

    @pl.when(has_s)
    def _():
        away_se.wait_send()
        away_sw.wait_send()
        away_s.wait_send()


def store_kernel(count, *refs):
    sems = refs[-1]
    copies = [pltpu.make_async_copy(refs[k], refs[count + k], sems.at[k]) for k in range(count)]
    for one in copies:
        one.start()
    for one in copies:
        one.wait()


def local(sea_level, transport_u, transport_v, ocean_depth, tracers, land_mask):
    rows, cols = sea_level.shape
    f32 = jnp.float32
    plane, pair = jax.ShapeDtypeStruct((rows, cols), f32), jax.ShapeDtypeStruct((2, rows, cols), f32)
    shapes = [plane, plane, plane, pair]
    anywhere, vmem = pl.BlockSpec(memory_space=pl.ANY), pl.BlockSpec(memory_space=pltpu.VMEM)
    held = pl.pallas_call(
        exchange_kernel,
        out_shape=[MEM(s.shape, s.dtype) for s in shapes],
        in_specs=[anywhere] * 6,
        out_specs=[vmem] * 4,
        scratch_shapes=[
            pltpu.VMEM((FIELDS, rows + 16, cols), f32),
            pltpu.VMEM((rows, cols), jnp.int32),
            pltpu.VMEM((rows, 128), f32),
            pltpu.VMEM((128, rows), f32),
            pltpu.VMEM((2, 24, rows), f32),
            pltpu.VMEM((2, 24, cols), f32),
            pltpu.VMEM((2, 24, rows), f32),
            pltpu.VMEM((2, 24, cols), f32),
            pltpu.VMEM((4, 8, 128), f32),
            pltpu.VMEM((128, rows), f32),
            pltpu.VMEM((FIELDS, 32, cols + 128), f32),
            pltpu.VMEM((8, cols + 128), f32),
            pltpu.SemaphoreType.DMA((6,)),
            pltpu.SemaphoreType.DMA((8,)),
            pltpu.SemaphoreType.DMA((8,)),
        ],
        compiler_params=pltpu.CompilerParams(collective_id=0, has_side_effects=True, vmem_limit_bytes=32 * 2**20),
        name="exchange",
    )(sea_level, transport_u, transport_v, ocean_depth, tracers, land_mask)
    return pl.pallas_call(
        functools.partial(store_kernel, len(shapes)),
        out_shape=shapes,
        in_specs=[IN] * 4,
        out_specs=[anywhere] * 4,
        scratch_shapes=[pltpu.SemaphoreType.DMA((len(shapes),))],
        name="store",
    )(*held)


MEM = pltpu.VMEM
IN = pl.BlockSpec(memory_space=pltpu.VMEM)


def solution(mesh):
    spread, tracers = P("gy", "gx"), P(None, "gy", "gx")
    return jax.shard_map(
        local,
        mesh=mesh,
        in_specs=(spread, spread, spread, spread, tracers, spread),
        out_specs=(spread, spread, spread, tracers),
        check_vma=False,
    )
```

```python
import functools

import jax
import jax.numpy as jnp
from jax import lax
from jax.experimental import pallas as pl
from jax.experimental.pallas import tpu as pltpu
from jax.sharding import PartitionSpec as P

SUBSTEPS = 3
DIVERGENCE_STEP = 0.3
GRAVITY_STEP = 0.3
DRAG_RATE = 0.05
CORIOLIS_TOP = 0.4
ADVECT_STEP = 0.1

MESH = pl.DeviceIdType.MESH
FIELDS = 7
U, V, LEVEL, MASK, DEPTH, T0, T1 = range(FIELDS)
GROUP = 16
BLOCK = 32
W, E, S, N, SW, SE, NW, NE = range(8)


def roll(x, shift, axis):
    return pltpu.roll(x, shift % x.shape[axis], axis)


def lanes(shape):
    return lax.broadcasted_iota(jnp.int32, shape, 1)


def sublanes(shape):
    return lax.broadcasted_iota(jnp.int32, shape, 0)


def advance(u, v, level, mask, depth, tracers, cor_u, cor_v, row_axis, fold=None):
    col_axis = 1 - row_axis
    west = lambda x: roll(x, 1, col_axis)
    east = lambda x: roll(x, -1, col_axis)
    south = lambda x: roll(x, 1, row_axis)
    north = lambda x: roll(x, -1, row_axis)
    head = lambda x: x[:8]

    def sym(x, other):
        return jnp.concatenate([jnp.where(fold[0], 0.5 * (head(x) - other), head(x)), x[8:]], axis=0)

    east_mask = mask * east(mask)
    north_mask = mask * north(mask)
    depth_u = 0.5 * (depth + east(depth))
    depth_v = 0.5 * (depth + north(depth))
    keep_u = east_mask * (1.0 - DRAG_RATE / depth_u)
    keep_v = north_mask * (1.0 - DRAG_RATE / depth_v)
    push_u = east_mask * (GRAVITY_STEP * depth_u)
    push_v = north_mask * (GRAVITY_STEP * depth_v)
    turn_u = east_mask * (0.25 * cor_u)
    turn_v = north_mask * (0.25 * cor_v)
    spread = DIVERGENCE_STEP * mask
    u = east_mask * u
    v = north_mask * v
    if fold is not None:
        other = head(north_mask) * fold[1]
    for step in range(SUBSTEPS):
        if fold is not None:
            v, other = sym(v, other), 0.5 * (other - head(v))
        flow_west = west(u)
        pair = flow_west + u
        sym_south = south(v)
        level = level - spread * (u - flow_west + v - sym_south)
        both = v + sym_south
        pairs = pair + north(pair)
        slope_v = north(level) - level
        new_u = keep_u * u - push_u * (east(level) - level) + turn_u * (both + east(both))
        if fold is not None:
            other = head(keep_v) * other + head(push_v) * head(slope_v) + head(turn_v) * head(pairs)
        v = keep_v * v - push_v * slope_v - turn_v * pairs
        u = new_u
        sum_u = u if step == 0 else sum_u + u
        sum_v = v if step == 0 else sum_v + v
        if fold is not None:
            sum_other = other if step == 0 else sum_other + other
    mean_u = sum_u * (1.0 / SUBSTEPS)
    mean_v = sum_v * (1.0 / SUBSTEPS)
    if fold is not None:
        mean_v = sym(mean_v, sum_other * (1.0 / SUBSTEPS))
    out_u, in_u = jnp.maximum(mean_u, 0.0), jnp.minimum(mean_u, 0.0)
    out_v, in_v = jnp.maximum(mean_v, 0.0), jnp.minimum(mean_v, 0.0)
    rate = ADVECT_STEP * mask / depth
    new = []
    for t in tracers:
        flux_u = out_u * t + in_u * east(t)
        flux_v = out_v * t + in_v * north(t)
        new.append(t - rate * (flux_u - west(flux_u) + flux_v - south(flux_v)))
    return level, u, v, new[0], new[1]


def pack_last(narrow, wide, x):
    s = sublanes(x[0].shape)
    return [
        jnp.where(s < 1, roll(x[T0], 1, 0), jnp.where(s < 4, roll(x[narrow], 4, 0), x[wide])),
        jnp.where(s < 1, roll(x[T1], 1, 0), jnp.where(s < 4, roll(x[LEVEL], 4, 0), x[MASK])),
        x[DEPTH],
    ]


def pack_first(narrow, wide, x):
    s = sublanes(x[0].shape)
    return [
        jnp.where(s < 3, x[narrow], jnp.where(s < 4, roll(x[T0], 3, 0), roll(x[wide], 4, 0))),
        jnp.where(s < 3, x[LEVEL], jnp.where(s < 4, roll(x[T1], 3, 0), roll(x[MASK], 4, 0))),
        x[DEPTH],
    ]


def unpack_last(narrow, wide, a, b, c):
    x = {narrow: roll(a, 4, 0), wide: a, LEVEL: roll(b, 4, 0), MASK: b, DEPTH: c, T0: roll(a, 7, 0), T1: roll(b, 7, 0)}
    return [x[f] for f in range(FIELDS)]


def unpack_first(narrow, wide, a, b, c):
    x = {narrow: a, wide: roll(a, 4, 0), LEVEL: b, MASK: roll(b, 4, 0), DEPTH: c, T0: roll(a, 5, 0), T1: roll(b, 5, 0)}
    return [x[f] for f in range(FIELDS)]


def put_columns(ref, parts, last):
    a, b, c = parts
    half = c.shape[1] // 2
    left, right = c[:, :half], c[:, half:]
    upper = sublanes(left.shape) < 4
    both = jnp.where(upper, roll(left, 4, 0), right) if last else jnp.where(upper, left, roll(right, 4, 0))
    for k, part in enumerate([a[:, :half], a[:, half:], b[:, :half], b[:, half:], both]):
        ref[8 * k : 8 * k + 8] = part


def get_columns(ref, last):
    both = ref[32:40]
    left, right = (roll(both, 4, 0), both) if last else (both, roll(both, 4, 0))
    pairs = [(ref[0:8], ref[8:16]), (ref[16:24], ref[24:32]), (left, right)]
    return [jnp.concatenate(pair, axis=1) for pair in pairs]


def pack_corner(x, first_row, first_lane):
    row, lane = sublanes(x.shape), lanes(x.shape)
    total = jnp.zeros_like(x)
    for r in range(4):
        here = (row == first_row + r) & (lane & 12 == 4 * r)
        total = total + jnp.where(here, roll(x, 4 * r - first_lane, 1), 0.0)
    return jnp.sum(total, axis=0, keepdims=True)


def unpack_corner(x, first_row, first_lane, base):
    x = jnp.broadcast_to(x, (8, 128))
    row, lane = sublanes(x.shape), lanes(x.shape)
    for r in range(4):
        here = (row == first_row + r) & (lane & 12 == first_lane)
        base = jnp.where(here, roll(x, first_lane - 4 * r, 1), base)
    return base


def flip(x, axis, group):
    at = lax.broadcasted_iota(jnp.int32, x.shape, axis)
    bit = 1
    while bit < group:
        x = jnp.where(at & bit == 0, roll(x, -bit, axis), roll(x, bit, axis))
        bit *= 2
    return x


def exchange_kernel(
    level_in, u_in, v_in, depth_in, tracers_in, land_in,
    level_out, u_out, v_out, tracers_out,
    x, land, packed, packed_t, send_cols, send_rows, send_corners, got_cols, got_rows, got_corners, halo_t, strip, other,
    load_sem, send_sem, recv_sem,
):
    rows, cols = u_out.shape
    nx, ny = lax.axis_size("gx"), lax.axis_size("gy")
    me_x, me_y = lax.axis_index("gx"), lax.axis_index("gy")
    to_e, to_w = lax.rem(me_x + 1, nx), lax.rem(me_x + nx - 1, nx)
    top, bottom = me_y == ny - 1, me_y == 0
    past = lambda column: jnp.where(top, nx - 1 - column, column)
    to_n, to_s = jnp.where(top, me_y, me_y + 1), jnp.where(bottom, me_y, me_y - 1)
    own_ne, own_nw = top & (past(to_e) == me_x), top & (past(to_w) == me_x)
    has_s = jnp.logical_not(bottom)

    barrier = pltpu.get_barrier_semaphore()

    def greet(to_x, to_y):
        pl.semaphore_signal(barrier, inc=1, device_id=(to_x, to_y), device_id_type=MESH)

    greet(to_w, me_y)
    greet(to_e, me_y)
    greet(past(me_x), to_n)
    pl.when(jnp.logical_not(own_ne))(lambda: greet(past(to_e), to_n))
    pl.when(jnp.logical_not(own_nw))(lambda: greet(past(to_w), to_n))

    @pl.when(has_s)
    def _():
        greet(me_x, to_s)
        greet(to_e, to_s)
        greet(to_w, to_s)

    inner = pl.ds(8, rows)
    loads = [
        pltpu.make_async_copy(land_in, land, load_sem.at[0]),
        pltpu.make_async_copy(u_in, x.at[U, inner], load_sem.at[1]),
        pltpu.make_async_copy(v_in, x.at[V, inner], load_sem.at[2]),
        pltpu.make_async_copy(level_in, x.at[LEVEL, inner], load_sem.at[3]),
        pltpu.make_async_copy(depth_in, x.at[DEPTH, inner], load_sem.at[4]),
        pltpu.make_async_copy(tracers_in, x.at[pl.ds(T0, 2), inner], load_sem.at[5]),
    ]
    for load in loads:
        load.start()
    for f in range(FIELDS):
        x[f, 0:8] = jnp.ones((8, cols), jnp.float32)
        x[f, rows + 8 : rows + 16] = jnp.ones((8, cols), jnp.float32)
    for load in loads:
        load.wait()

    size = 64

    def pack_columns(k, carry):
        at = pl.multiple_of(k * size, size)
        x[MASK, pl.ds(at + 8, size)] = land[pl.ds(at, size)].astype(jnp.float32)
        lane = lanes((size, 128))
        result = None
        for f in range(FIELDS):
            first = x[f, pl.ds(at + 8, size), 0:128]
            last = x[f, pl.ds(at + 8, size), cols - 128 : cols]
            ends = roll(jnp.where(lane < 64, first, last), f * GROUP + 8, 1)
            result = ends if f == 0 else jnp.where(lane < f * GROUP, result, ends)
        packed[pl.ds(at, size)] = result
        return carry

    lax.fori_loop(0, rows // size, pack_columns, 0, unroll=True)
    packed_t[...] = packed[...].T

    groups = [GROUP * f for f in range(FIELDS)]
    north_end, south_end = packed[rows - 8 : rows], packed[0:8]
    send_corners[NE - SW] = pack_corner(north_end, 4, 4)
    send_corners[NW - SW] = pack_corner(north_end, 4, 8)
    send_corners[SE - SW] = pack_corner(south_end, 0, 4)
    send_corners[SW - SW] = pack_corner(south_end, 0, 8)
    put_columns(send_cols.at[0], pack_last(V, U, [packed_t[g : g + 8] for g in groups]), True)
    put_columns(send_cols.at[1], pack_first(V, U, [packed_t[g + 8 : g + 16] for g in groups]), False)
    send_rows[0] = jnp.concatenate(pack_last(U, V, [x[f, rows : rows + 8] for f in range(FIELDS)]), axis=0)
    send_rows[1] = jnp.concatenate(pack_first(U, V, [x[f, 8:16] for f in range(FIELDS)]), axis=0)

    def coriolis(row):
        row = row.astype(jnp.float32)
        total = 1.0 * ny * rows
        return CORIOLIS_TOP * ((row + 0.5) / total), CORIOLIS_TOP * ((row + 1.0) / total)

    def compute_inner(k, carry):
        at = pl.multiple_of(k * BLOCK, BLOCK)
        part = [x[f, pl.ds(at, BLOCK + 16)] for f in range(FIELDS)]
        row = me_y * rows + at - 8 + sublanes((BLOCK + 16, 1))
        out = advance(*part[:5], part[5:], *coriolis(row), 0)
        keep = pl.ds(at, BLOCK)
        level_out[keep] = out[0][8 : BLOCK + 8]
        u_out[keep] = out[1][8 : BLOCK + 8]
        v_out[keep] = out[2][8 : BLOCK + 8]
        tracers_out[0, keep] = out[3][8 : BLOCK + 8]
        tracers_out[1, keep] = out[4][8 : BLOCK + 8]
        return carry

    blocks = rows // BLOCK
    sends_first = lax.rem(me_x, 2)
    lax.fori_loop(0, blocks * (1 - sends_first), compute_inner, 0)

    def copy(source, target, k, at, to_x, to_y):
        return pltpu.make_async_remote_copy(
            src_ref=source,
            dst_ref=target,
            send_sem=send_sem.at[k],
            recv_sem=recv_sem.at[at],
            device_id=(to_x, to_y),
            device_id_type=MESH,
        )

    def corner(k, at, to_x, to_y):
        return copy(send_corners.at[k - SW], got_corners.at[at - SW], k, at, to_x, to_y)

    away_e = copy(send_cols.at[0], got_cols.at[0], E, W, to_e, me_y)
    away_w = copy(send_cols.at[1], got_cols.at[1], W, E, to_w, me_y)
    away_s = copy(send_rows.at[1], got_rows.at[1], S, N, me_x, to_s)
    away_n = copy(send_rows.at[0], got_rows.at[0], N, S, me_x, to_n)
    fold_n = copy(send_rows.at[0], got_rows.at[1], N, N, past(me_x), to_n)
    away_se, away_sw = corner(SE, NW, to_e, to_s), corner(SW, NE, to_w, to_s)
    away_ne, away_nw = corner(NE, SW, to_e, to_n), corner(NW, SE, to_w, to_n)
    fold_ne, fold_nw = corner(NE, NE, past(to_e), to_n), corner(NW, NW, past(to_w), to_n)
    not_top = jnp.logical_not(top)
    far_ne, far_nw = top & jnp.logical_not(own_ne), top & jnp.logical_not(own_nw)

    count = 3 + jnp.where(own_ne, 0, 1) + jnp.where(own_nw, 0, 1) + jnp.where(has_s, 3, 0)
    pl.semaphore_wait(barrier, count)

    @pl.when(not_top)
    def _():
        away_n.start()
        away_ne.start()
        away_nw.start()

    pl.when(top)(lambda: fold_n.start())
    pl.when(far_ne)(lambda: fold_ne.start())
    pl.when(far_nw)(lambda: fold_nw.start())

    @pl.when(has_s)
    def _():
        away_s.start()
        away_se.start()
        away_sw.start()

    away_e.start()
    away_w.start()

    lax.fori_loop(blocks * (1 - sends_first), blocks, compute_inner, 0)

    away_w.wait_recv()
    away_e.wait_recv()
    away_s.wait_recv()

    @pl.when(has_s)
    def _():
        away_n.wait_recv()
        away_ne.wait_recv()
        away_nw.wait_recv()

    pl.when(jnp.logical_not(own_nw))(lambda: away_se.wait_recv())
    pl.when(jnp.logical_not(own_ne))(lambda: away_sw.wait_recv())

    @pl.when(own_nw)
    def _():
        got_corners[NW - SW] = send_corners[NW - SW]

    @pl.when(own_ne)
    def _():
        got_corners[NE - SW] = send_corners[NE - SW]

    from_w = unpack_last(V, U, *get_columns(got_cols.at[0], True))
    from_e = unpack_first(V, U, *get_columns(got_cols.at[1], False))
    for f, g in enumerate(groups):
        halo_t[g : g + 8] = from_w[f]
        halo_t[g + 8 : g + 16] = from_e[f]
    halo_t[GROUP * FIELDS :] = jnp.ones((128 - GROUP * FIELDS, rows), jnp.float32)

    def put_rows(at, parts, sides):
        for f in range(FIELDS):
            strip[f, at : at + 8, 0:cols] = parts[f]
            strip[f, at : at + 8, cols : cols + 128] = roll(sides, -(GROUP * f + 8), 1)

    put_rows(0, [x[f, rows : rows + 8] for f in range(FIELDS)], halo_t[:, rows - 128 : rows].T[120:128])
    put_rows(24, [x[f, 8:16] for f in range(FIELDS)], halo_t[:, 0:128].T[0:8])
    from_n, from_s = ([ref[0:8], ref[8:16], ref[16:24]] for ref in (got_rows.at[1], got_rows.at[0]))
    from_ne, from_nw, from_se, from_sw = (got_corners[k - SW] for k in (NE, NW, SE, SW))
    nothing = jnp.zeros((8, 128), jnp.float32)

    @pl.when(not_top)
    def _():
        sides = unpack_corner(from_ne, 0, 8, unpack_corner(from_nw, 0, 4, nothing))
        put_rows(8, unpack_first(U, V, *from_n), sides)
        other[...] = jnp.zeros_like(other)

    @pl.when(top)
    def _():
        parts = [flip(part, 0, 8) for part in unpack_last(U, V, *from_n)]
        tiles = range(0, cols, 128)
        parts = [
            jnp.concatenate([flip(part[:, c : c + 128], 1, 128) for c in reversed(tiles)], axis=1)
            for part in parts
        ]
        sides = unpack_corner(flip(from_nw, 1, GROUP), 0, 4, nothing)
        put_rows(8, parts, unpack_corner(flip(from_ne, 1, GROUP), 0, 8, sides))
        strip[U, 8:16] = -roll(strip[U, 8:16], -1, 1)
        mirrored = strip[V, 8:16]
        strip[V, 8:16] = -roll(mirrored, -1, 0)
        other[...] = roll(mirrored, -1, 0)

    @pl.when(has_s)
    def _():
        sides = unpack_corner(from_se, 4, 8, unpack_corner(from_sw, 4, 4, nothing))
        put_rows(16, unpack_last(U, V, *from_s), sides)

    @pl.when(bottom)
    def _():
        for f in range(FIELDS):
            strip[f, 16:24] = jnp.full((8, cols + 128), 1.0 if f == DEPTH else 0.0, jnp.float32)

    upper = sublanes((8, rows)) < 4
    parts = [
        jnp.concatenate(
            [packed_t[g : g + 8], jnp.where(upper, halo_t[g + 8 : g + 16], halo_t[g : g + 8]), packed_t[g + 8 : g + 16]],
            axis=0,
        )
        for g in groups
    ]
    row = me_y * rows + lanes((1, rows))
    by_col = advance(*parts[:5], parts[5:], *coriolis(row), 1)

    s = sublanes((24, 1))
    row = me_y * rows + jnp.where(s < 12, rows - 8 + s, s - 16)
    total = ny * rows
    cor_u = coriolis(jnp.where(row >= total, 2 * total - 1 - row, row))[0]
    cor_v = coriolis(jnp.where(row >= total, 2 * total - 2 - row, row))[1]
    upper = sublanes((8, cols + 128)) < 4
    parts = [
        jnp.concatenate([strip[f, 0:8], jnp.where(upper, strip[f, 8:16], strip[f, 16:24]), strip[f, 24:32]], axis=0)
        for f in range(FIELDS)
    ]
    at_fold = top & (sublanes((8, cols + 128)) == 7)
    by_row = advance(*parts[:5], parts[5:], cor_u, cor_v, 0, (at_fold, other[...]))

    zeros = jnp.zeros((128 - GROUP * 5, rows), jnp.float32)
    back = jnp.concatenate([part for o in by_col for part in (o[0:8], o[16:24])] + [zeros], axis=0).T
    outs = [level_out, u_out, v_out, tracers_out.at[0], tracers_out.at[1]]
    lane = lanes((rows, 128))
    s = sublanes((8, cols))
    for o, out in enumerate(outs):
        ends = roll(back, -(GROUP * o + 8), 1)
        out[:, 0:128] = jnp.where(lane < 4, ends, out[:, 0:128])
        out[:, cols - 128 : cols] = jnp.where(lane >= 124, ends, out[:, cols - 128 : cols])
        out[0:8] = jnp.where(s < 4, by_row[o][16:24, 0:cols], out[0:8])
        out[rows - 8 : rows] = jnp.where(s >= 4, by_row[o][0:8, 0:cols], out[rows - 8 : rows])

    away_e.wait_send()
    away_w.wait_send()

    @pl.when(not_top)
    def _():
        away_ne.wait_send()
        away_nw.wait_send()
        away_n.wait_send()

    @pl.when(top)
    def _():
        fold_n.wait_send()

    pl.when(far_ne)(lambda: fold_ne.wait_send())
    pl.when(far_nw)(lambda: fold_nw.wait_send())

    @pl.when(has_s)
    def _():
        away_se.wait_send()
        away_sw.wait_send()
        away_s.wait_send()


def store_kernel(count, *refs):
    sems = refs[-1]
    copies = [pltpu.make_async_copy(refs[k], refs[count + k], sems.at[k]) for k in range(count)]
    for one in copies:
        one.start()
    for one in copies:
        one.wait()


def local(*arguments):
    rows, cols = arguments[0].shape
    f32 = jnp.float32
    plane, pair = jax.ShapeDtypeStruct((rows, cols), f32), jax.ShapeDtypeStruct((2, rows, cols), f32)
    shapes = [plane, plane, plane, pair]
    anywhere, vmem = pl.BlockSpec(memory_space=pl.ANY), pl.BlockSpec(memory_space=pltpu.VMEM)
    held = pl.pallas_call(
        exchange_kernel,
        out_shape=[MEM(s.shape, s.dtype) for s in shapes],
        in_specs=[anywhere] * 6,
        out_specs=[vmem] * 4,
        scratch_shapes=[
            pltpu.VMEM((FIELDS, rows + 16, cols), f32),
            pltpu.VMEM((rows, cols), jnp.int32),
            pltpu.VMEM((rows, 128), f32),
            pltpu.VMEM((128, rows), f32),
            pltpu.VMEM((2, 40, rows // 2), f32),
            pltpu.VMEM((2, 24, cols), f32),
            pltpu.VMEM((4, 1, 128), f32),
            pltpu.VMEM((2, 40, rows // 2), f32),
            pltpu.VMEM((2, 24, cols), f32),
            pltpu.VMEM((4, 1, 128), f32),
            pltpu.VMEM((128, rows), f32),
            pltpu.VMEM((FIELDS, 32, cols + 128), f32),
            pltpu.VMEM((8, cols + 128), f32),
            pltpu.SemaphoreType.DMA((6,)),
            pltpu.SemaphoreType.DMA((8,)),
            pltpu.SemaphoreType.DMA((8,)),
        ],
        compiler_params=pltpu.CompilerParams(collective_id=0, has_side_effects=True, vmem_limit_bytes=32 * 2**20),
        name="exchange",
    )(*(pltpu.with_memory_space_constraint(a, pltpu.HBM) for a in arguments))
    return pl.pallas_call(
        functools.partial(store_kernel, len(shapes)),
        out_shape=shapes,
        in_specs=[IN] * 4,
        out_specs=[anywhere] * 4,
        scratch_shapes=[pltpu.SemaphoreType.DMA((len(shapes),))],
        name="store",
    )(*(pltpu.with_memory_space_constraint(a, pltpu.VMEM) for a in held))


MEM = pltpu.VMEM
IN = pl.BlockSpec(memory_space=pltpu.VMEM)


def solution(mesh):
    spread, tracers = P("gy", "gx"), P(None, "gy", "gx")
    return jax.shard_map(
        local,
        mesh=mesh,
        in_specs=(spread, spread, spread, spread, tracers, spread),
        out_specs=(spread, spread, spread, tracers),
        check_vma=False,
    )
```

```python
import functools

import jax
import jax.numpy as jnp
from jax import lax
from jax.experimental import pallas as pl
from jax.experimental.pallas import tpu as pltpu
from jax.sharding import PartitionSpec as P

SUBSTEPS = 3
DIVERGENCE_STEP = 0.3
GRAVITY_STEP = 0.3
DRAG_RATE = 0.05
CORIOLIS_TOP = 0.4
ADVECT_STEP = 0.1

MESH = pl.DeviceIdType.MESH
FIELDS = 7
U, V, LEVEL, MASK, DEPTH, T0, T1 = range(FIELDS)
GROUP = 16
BLOCK = 32
W, E, S, N, SW, SE, NW, NE = range(8)


def roll(x, shift, axis):
    return pltpu.roll(x, shift % x.shape[axis], axis)


def lanes(shape):
    return lax.broadcasted_iota(jnp.int32, shape, 1)


def sublanes(shape):
    return lax.broadcasted_iota(jnp.int32, shape, 0)


def advance(u, v, level, mask, depth, tracers, cor_u, cor_v, row_axis, fold=None):
    col_axis = 1 - row_axis
    west = lambda x: roll(x, 1, col_axis)
    east = lambda x: roll(x, -1, col_axis)
    south = lambda x: roll(x, 1, row_axis)
    north = lambda x: roll(x, -1, row_axis)
    head = lambda x: x[:8]

    def sym(x, other):
        return jnp.concatenate([jnp.where(fold[0], 0.5 * (head(x) - other), head(x)), x[8:]], axis=0)

    east_mask = mask * east(mask)
    north_mask = mask * north(mask)
    depth_u = 0.5 * (depth + east(depth))
    depth_v = 0.5 * (depth + north(depth))
    keep_u = east_mask * (1.0 - DRAG_RATE / depth_u)
    keep_v = north_mask * (1.0 - DRAG_RATE / depth_v)
    push_u = east_mask * (GRAVITY_STEP * depth_u)
    push_v = north_mask * (GRAVITY_STEP * depth_v)
    turn_u = east_mask * (0.25 * cor_u)
    turn_v = north_mask * (0.25 * cor_v)
    spread = DIVERGENCE_STEP * mask
    u = east_mask * u
    v = north_mask * v
    if fold is not None:
        other = head(north_mask) * fold[1]
    for step in range(SUBSTEPS):
        if fold is not None:
            v, other = sym(v, other), 0.5 * (other - head(v))
        flow_west = west(u)
        pair = flow_west + u
        sym_south = south(v)
        level = level - spread * (u - flow_west + v - sym_south)
        both = v + sym_south
        pairs = pair + north(pair)
        slope_v = north(level) - level
        new_u = keep_u * u - push_u * (east(level) - level) + turn_u * (both + east(both))
        if fold is not None:
            other = head(keep_v) * other + head(push_v) * head(slope_v) + head(turn_v) * head(pairs)
        v = keep_v * v - push_v * slope_v - turn_v * pairs
        u = new_u
        sum_u = u if step == 0 else sum_u + u
        sum_v = v if step == 0 else sum_v + v
        if fold is not None:
            sum_other = other if step == 0 else sum_other + other
    mean_u = sum_u * (1.0 / SUBSTEPS)
    mean_v = sum_v * (1.0 / SUBSTEPS)
    if fold is not None:
        mean_v = sym(mean_v, sum_other * (1.0 / SUBSTEPS))
    out_u, in_u = jnp.maximum(mean_u, 0.0), jnp.minimum(mean_u, 0.0)
    out_v, in_v = jnp.maximum(mean_v, 0.0), jnp.minimum(mean_v, 0.0)
    rate = ADVECT_STEP * mask / depth
    new = []
    for t in tracers:
        flux_u = out_u * t + in_u * east(t)
        flux_v = out_v * t + in_v * north(t)
        new.append(t - rate * (flux_u - west(flux_u) + flux_v - south(flux_v)))
    return level, u, v, new[0], new[1]


def pack_last(narrow, wide, x):
    s = sublanes(x[0].shape)
    return [
        jnp.where(s < 1, roll(x[T0], 1, 0), jnp.where(s < 4, roll(x[narrow], 4, 0), x[wide])),
        jnp.where(s < 1, roll(x[T1], 1, 0), jnp.where(s < 4, roll(x[LEVEL], 4, 0), x[MASK])),
        x[DEPTH],
    ]


def pack_first(narrow, wide, x):
    s = sublanes(x[0].shape)
    return [
        jnp.where(s < 3, x[narrow], jnp.where(s < 4, roll(x[T0], 3, 0), roll(x[wide], 4, 0))),
        jnp.where(s < 3, x[LEVEL], jnp.where(s < 4, roll(x[T1], 3, 0), roll(x[MASK], 4, 0))),
        x[DEPTH],
    ]


def unpack_last(narrow, wide, a, b, c):
    x = {narrow: roll(a, 4, 0), wide: a, LEVEL: roll(b, 4, 0), MASK: b, DEPTH: c, T0: roll(a, 7, 0), T1: roll(b, 7, 0)}
    return [x[f] for f in range(FIELDS)]


def unpack_first(narrow, wide, a, b, c):
    x = {narrow: a, wide: roll(a, 4, 0), LEVEL: b, MASK: roll(b, 4, 0), DEPTH: c, T0: roll(a, 5, 0), T1: roll(b, 5, 0)}
    return [x[f] for f in range(FIELDS)]


def put_columns(ref, parts, last):
    a, b, c = parts
    half = c.shape[1] // 2
    left, right = c[:, :half], c[:, half:]
    upper = sublanes(left.shape) < 4
    both = jnp.where(upper, roll(left, 4, 0), right) if last else jnp.where(upper, left, roll(right, 4, 0))
    for k, part in enumerate([a[:, :half], a[:, half:], b[:, :half], b[:, half:], both]):
        ref[8 * k : 8 * k + 8] = part


def get_columns(ref, last):
    both = ref[32:40]
    left, right = (roll(both, 4, 0), both) if last else (both, roll(both, 4, 0))
    pairs = [(ref[0:8], ref[8:16]), (ref[16:24], ref[24:32]), (left, right)]
    return [jnp.concatenate(pair, axis=1) for pair in pairs]


def pack_corner(x, first_row, first_lane):
    row, lane = sublanes(x.shape), lanes(x.shape)
    total = jnp.zeros_like(x)
    for r in range(4):
        here = (row == first_row + r) & (lane & 12 == 4 * r)
        total = total + jnp.where(here, roll(x, 4 * r - first_lane, 1), 0.0)
    return jnp.sum(total, axis=0, keepdims=True)


def unpack_corner(x, first_row, first_lane, base):
    x = jnp.broadcast_to(x, (8, 128))
    row, lane = sublanes(x.shape), lanes(x.shape)
    for r in range(4):
        here = (row == first_row + r) & (lane & 12 == first_lane)
        base = jnp.where(here, roll(x, first_lane - 4 * r, 1), base)
    return base


def flip(x, axis, group):
    at = lax.broadcasted_iota(jnp.int32, x.shape, axis)
    bit = 1
    while bit < group:
        x = jnp.where(at & bit == 0, roll(x, -bit, axis), roll(x, bit, axis))
        bit *= 2
    return x


def exchange_kernel(
    level_in, u_in, v_in, depth_in, tracers_in, land_in,
    level_out, u_out, v_out, tracers_out,
    x, land, packed, packed_t, send_cols, send_rows, send_corners, got_cols, got_rows, got_corners, halo_t, strip, other,
    load_sem, send_sem, recv_sem,
):
    rows, cols = u_out.shape
    nx, ny = lax.axis_size("gx"), lax.axis_size("gy")
    me_x, me_y = lax.axis_index("gx"), lax.axis_index("gy")
    to_e, to_w = lax.rem(me_x + 1, nx), lax.rem(me_x + nx - 1, nx)
    top, bottom = me_y == ny - 1, me_y == 0
    past = lambda column: jnp.where(top, nx - 1 - column, column)
    to_n, to_s = jnp.where(top, me_y, me_y + 1), jnp.where(bottom, me_y, me_y - 1)
    own_ne, own_nw = top & (past(to_e) == me_x), top & (past(to_w) == me_x)
    has_s = jnp.logical_not(bottom)

    barrier = pltpu.get_barrier_semaphore()

    def greet(to_x, to_y):
        pl.semaphore_signal(barrier, inc=1, device_id=(to_x, to_y), device_id_type=MESH)

    greet(to_w, me_y)
    greet(to_e, me_y)
    greet(past(me_x), to_n)
    pl.when(jnp.logical_not(own_ne))(lambda: greet(past(to_e), to_n))
    pl.when(jnp.logical_not(own_nw))(lambda: greet(past(to_w), to_n))

    @pl.when(has_s)
    def _():
        greet(me_x, to_s)
        greet(to_e, to_s)
        greet(to_w, to_s)

    inner = pl.ds(8, rows)
    arguments = [
        (u_in, x.at[U, inner]),
        (v_in, x.at[V, inner]),
        (level_in, x.at[LEVEL, inner]),
        (land_in, land),
        (depth_in, x.at[DEPTH, inner]),
        (tracers_in, x.at[pl.ds(T0, 2), inner]),
    ]

    def load(at, k, columns):
        source, target = arguments[k]
        where = (slice(None),) * (len(source.shape) - 1) + (columns,)
        return pltpu.make_async_copy(source.at[where], target.at[where], load_sem.at[at, k])

    ends = (pl.ds(0, 128), pl.ds(cols - 128, 128))
    end_loads = [[load(at, k, columns) for at, columns in enumerate(ends)] for k in range(len(arguments))]
    middle = pl.ds(128, cols - 256)
    middle_loads = [load(2, k, middle) for k in range(len(arguments))] if cols > 256 else []
    for one in [one for pair in end_loads for one in pair] + middle_loads:
        one.start()
    for f in range(FIELDS):
        x[f, 0:8] = jnp.ones((8, cols), jnp.float32)
        x[f, rows + 8 : rows + 16] = jnp.ones((8, cols), jnp.float32)

    lane = lanes((rows, 128))
    for f in range(FIELDS):
        if f != T1:
            for one in end_loads[f]:
                one.wait()
        if f == MASK:
            first, last = (land[:, columns].astype(jnp.float32) for columns in ends)
        else:
            first, last = (x[f, inner, columns] for columns in ends)
        both = roll(jnp.where(lane < 64, first, last), f * GROUP + 8, 1)
        packed[...] = both if f == 0 else jnp.where(lane < f * GROUP, packed[...], both)
    packed_t[...] = packed[...].T

    groups = [GROUP * f for f in range(FIELDS)]
    north_end, south_end = packed[rows - 8 : rows], packed[0:8]
    send_corners[NE - SW] = pack_corner(north_end, 4, 4)
    send_corners[NW - SW] = pack_corner(north_end, 4, 8)
    send_corners[SE - SW] = pack_corner(south_end, 0, 4)
    send_corners[SW - SW] = pack_corner(south_end, 0, 8)
    put_columns(send_cols.at[0], pack_last(V, U, [packed_t[g : g + 8] for g in groups]), True)
    put_columns(send_cols.at[1], pack_first(V, U, [packed_t[g + 8 : g + 16] for g in groups]), False)

    def copy(source, target, k, at, to_x, to_y):
        return pltpu.make_async_remote_copy(
            src_ref=source,
            dst_ref=target,
            send_sem=send_sem.at[k],
            recv_sem=recv_sem.at[at],
            device_id=(to_x, to_y),
            device_id_type=MESH,
        )

    def corner(k, at, to_x, to_y):
        return copy(send_corners.at[k - SW], got_corners.at[at - SW], k, at, to_x, to_y)

    away_e = copy(send_cols.at[0], got_cols.at[0], E, W, to_e, me_y)
    away_w = copy(send_cols.at[1], got_cols.at[1], W, E, to_w, me_y)
    away_s = copy(send_rows.at[1], got_rows.at[1], S, N, me_x, to_s)
    away_n = copy(send_rows.at[0], got_rows.at[0], N, S, me_x, to_n)
    fold_n = copy(send_rows.at[0], got_rows.at[1], N, N, past(me_x), to_n)
    away_se, away_sw = corner(SE, NW, to_e, to_s), corner(SW, NE, to_w, to_s)
    away_ne, away_nw = corner(NE, SW, to_e, to_n), corner(NW, SE, to_w, to_n)
    fold_ne, fold_nw = corner(NE, NE, past(to_e), to_n), corner(NW, NW, past(to_w), to_n)
    not_top = jnp.logical_not(top)
    far_ne, far_nw = top & jnp.logical_not(own_ne), top & jnp.logical_not(own_nw)

    count = 3 + jnp.where(own_ne, 0, 1) + jnp.where(own_nw, 0, 1) + jnp.where(has_s, 3, 0)
    def send_far():
        @pl.when(not_top)
        def _():
            away_ne.start()
            away_nw.start()

        pl.when(far_ne)(lambda: fold_ne.start())
        pl.when(far_nw)(lambda: fold_nw.start())

        @pl.when(has_s)
        def _():
            away_se.start()
            away_sw.start()

        away_e.start()
        away_w.start()

    def send_near():
        pl.when(not_top)(lambda: away_n.start())
        pl.when(top)(lambda: fold_n.start())
        pl.when(has_s)(lambda: away_s.start())

    odd = lax.rem(me_x, 2)

    @pl.when(odd == 1)
    def _():
        pl.semaphore_wait(barrier, count)
        send_far()

    for one in middle_loads:
        one.wait()
    x[MASK, inner] = land[...].astype(jnp.float32)
    send_rows[0] = jnp.concatenate(pack_last(U, V, [x[f, rows : rows + 8] for f in range(FIELDS)]), axis=0)
    send_rows[1] = jnp.concatenate(pack_first(U, V, [x[f, 8:16] for f in range(FIELDS)]), axis=0)
    pl.when(odd == 1)(send_near)

    def coriolis(row):
        row = row.astype(jnp.float32)
        total = 1.0 * ny * rows
        return CORIOLIS_TOP * ((row + 0.5) / total), CORIOLIS_TOP * ((row + 1.0) / total)

    def compute_inner(k, carry):
        at = pl.multiple_of(k * BLOCK, BLOCK)
        part = [x[f, pl.ds(at, BLOCK + 16)] for f in range(FIELDS)]
        row = me_y * rows + at - 8 + sublanes((BLOCK + 16, 1))
        out = advance(*part[:5], part[5:], *coriolis(row), 0)
        keep = pl.ds(at, BLOCK)
        level_out[keep] = out[0][8 : BLOCK + 8]
        u_out[keep] = out[1][8 : BLOCK + 8]
        v_out[keep] = out[2][8 : BLOCK + 8]
        tracers_out[0, keep] = out[3][8 : BLOCK + 8]
        tracers_out[1, keep] = out[4][8 : BLOCK + 8]
        return carry

    blocks = rows // BLOCK
    lax.fori_loop(0, blocks * (1 - odd), compute_inner, 0)

    @pl.when(odd == 0)
    def _():
        pl.semaphore_wait(barrier, count)
        send_near()
        send_far()

    lax.fori_loop(blocks * (1 - odd), blocks, compute_inner, 0)

    away_w.wait_recv()
    away_e.wait_recv()
    away_s.wait_recv()

    @pl.when(has_s)
    def _():
        away_n.wait_recv()
        away_ne.wait_recv()
        away_nw.wait_recv()

    pl.when(jnp.logical_not(own_nw))(lambda: away_se.wait_recv())
    pl.when(jnp.logical_not(own_ne))(lambda: away_sw.wait_recv())

    @pl.when(own_nw)
    def _():
        got_corners[NW - SW] = send_corners[NW - SW]

    @pl.when(own_ne)
    def _():
        got_corners[NE - SW] = send_corners[NE - SW]

    from_w = unpack_last(V, U, *get_columns(got_cols.at[0], True))
    from_e = unpack_first(V, U, *get_columns(got_cols.at[1], False))
    for f, g in enumerate(groups):
        halo_t[g : g + 8] = from_w[f]
        halo_t[g + 8 : g + 16] = from_e[f]
    halo_t[GROUP * FIELDS :] = jnp.ones((128 - GROUP * FIELDS, rows), jnp.float32)

    def put_rows(at, parts, sides):
        for f in range(FIELDS):
            strip[f, at : at + 8, 0:cols] = parts[f]
            strip[f, at : at + 8, cols : cols + 128] = roll(sides, -(GROUP * f + 8), 1)

    put_rows(0, [x[f, rows : rows + 8] for f in range(FIELDS)], halo_t[:, rows - 128 : rows].T[120:128])
    put_rows(24, [x[f, 8:16] for f in range(FIELDS)], halo_t[:, 0:128].T[0:8])
    from_n, from_s = ([ref[0:8], ref[8:16], ref[16:24]] for ref in (got_rows.at[1], got_rows.at[0]))
    from_ne, from_nw, from_se, from_sw = (got_corners[k - SW] for k in (NE, NW, SE, SW))
    nothing = jnp.zeros((8, 128), jnp.float32)

    sides = unpack_corner(from_ne, 0, 8, unpack_corner(from_nw, 0, 4, nothing))
    put_rows(8, unpack_first(U, V, *from_n), sides)
    other[...] = jnp.zeros_like(other)
    sides = unpack_corner(from_se, 4, 8, unpack_corner(from_sw, 4, 4, nothing))
    put_rows(16, unpack_last(U, V, *from_s), sides)

    @pl.when(top)
    def _():
        parts = [flip(part, 0, 8) for part in unpack_last(U, V, *from_n)]
        tiles = range(0, cols, 128)
        parts = [
            jnp.concatenate([flip(part[:, c : c + 128], 1, 128) for c in reversed(tiles)], axis=1)
            for part in parts
        ]
        sides = unpack_corner(flip(from_nw, 1, GROUP), 0, 4, nothing)
        put_rows(8, parts, unpack_corner(flip(from_ne, 1, GROUP), 0, 8, sides))
        strip[U, 8:16] = -roll(strip[U, 8:16], -1, 1)
        mirrored = strip[V, 8:16]
        strip[V, 8:16] = -roll(mirrored, -1, 0)
        other[...] = roll(mirrored, -1, 0)

    @pl.when(bottom)
    def _():
        for f in range(FIELDS):
            strip[f, 16:24] = jnp.full((8, cols + 128), 1.0 if f == DEPTH else 0.0, jnp.float32)

    upper = sublanes((8, rows)) < 4
    parts = [
        jnp.concatenate(
            [packed_t[g : g + 8], jnp.where(upper, halo_t[g + 8 : g + 16], halo_t[g : g + 8]), packed_t[g + 8 : g + 16]],
            axis=0,
        )
        for g in groups
    ]
    row = me_y * rows + lanes((1, rows))
    by_col = advance(*parts[:5], parts[5:], *coriolis(row), 1)

    s = sublanes((24, 1))
    row = me_y * rows + jnp.where(s < 12, rows - 8 + s, s - 16)
    total = ny * rows
    cor_u = coriolis(jnp.where(row >= total, 2 * total - 1 - row, row))[0]
    cor_v = coriolis(jnp.where(row >= total, 2 * total - 2 - row, row))[1]
    upper = sublanes((8, cols + 128)) < 4
    parts = [
        jnp.concatenate([strip[f, 0:8], jnp.where(upper, strip[f, 8:16], strip[f, 16:24]), strip[f, 24:32]], axis=0)
        for f in range(FIELDS)
    ]
    at_fold = top & (sublanes((8, cols + 128)) == 7)
    by_row = advance(*parts[:5], parts[5:], cor_u, cor_v, 0, (at_fold, other[...]))

    zeros = jnp.zeros((128 - GROUP * 5, rows), jnp.float32)
    back = jnp.concatenate([part for o in by_col for part in (o[0:8], o[16:24])] + [zeros], axis=0).T
    outs = [level_out, u_out, v_out, tracers_out.at[0], tracers_out.at[1]]
    lane = lanes((rows, 128))
    s = sublanes((8, cols))
    for o, out in enumerate(outs):
        ends = roll(back, -(GROUP * o + 8), 1)
        out[:, 0:128] = jnp.where(lane < 4, ends, out[:, 0:128])
        out[:, cols - 128 : cols] = jnp.where(lane >= 124, ends, out[:, cols - 128 : cols])
        out[0:8] = jnp.where(s < 4, by_row[o][16:24, 0:cols], out[0:8])
        out[rows - 8 : rows] = jnp.where(s >= 4, by_row[o][0:8, 0:cols], out[rows - 8 : rows])

    away_e.wait_send()
    away_w.wait_send()

    @pl.when(not_top)
    def _():
        away_ne.wait_send()
        away_nw.wait_send()
        away_n.wait_send()

    @pl.when(top)
    def _():
        fold_n.wait_send()

    pl.when(far_ne)(lambda: fold_ne.wait_send())
    pl.when(far_nw)(lambda: fold_nw.wait_send())

    @pl.when(has_s)
    def _():
        away_se.wait_send()
        away_sw.wait_send()
        away_s.wait_send()


def store_kernel(count, *refs):
    sems = refs[-1]
    copies = [pltpu.make_async_copy(refs[k], refs[count + k], sems.at[k]) for k in range(count)]
    for one in copies:
        one.start()
    for one in copies:
        one.wait()


def local(*arguments):
    rows, cols = arguments[0].shape
    f32 = jnp.float32
    plane, pair = jax.ShapeDtypeStruct((rows, cols), f32), jax.ShapeDtypeStruct((2, rows, cols), f32)
    shapes = [plane, plane, plane, pair]
    anywhere, vmem = pl.BlockSpec(memory_space=pl.ANY), pl.BlockSpec(memory_space=pltpu.VMEM)
    held = pl.pallas_call(
        exchange_kernel,
        out_shape=[MEM(s.shape, s.dtype) for s in shapes],
        in_specs=[anywhere] * 6,
        out_specs=[vmem] * 4,
        scratch_shapes=[
            pltpu.VMEM((FIELDS, rows + 16, cols), f32),
            pltpu.VMEM((rows, cols), jnp.int32),
            pltpu.VMEM((rows, 128), f32),
            pltpu.VMEM((128, rows), f32),
            pltpu.VMEM((2, 40, rows // 2), f32),
            pltpu.VMEM((2, 24, cols), f32),
            pltpu.VMEM((4, 1, 128), f32),
            pltpu.VMEM((2, 40, rows // 2), f32),
            pltpu.VMEM((2, 24, cols), f32),
            pltpu.VMEM((4, 1, 128), f32),
            pltpu.VMEM((128, rows), f32),
            pltpu.VMEM((FIELDS, 32, cols + 128), f32),
            pltpu.VMEM((8, cols + 128), f32),
            pltpu.SemaphoreType.DMA((3, 6)),
            pltpu.SemaphoreType.DMA((8,)),
            pltpu.SemaphoreType.DMA((8,)),
        ],
        compiler_params=pltpu.CompilerParams(collective_id=0, has_side_effects=True, vmem_limit_bytes=32 * 2**20),
        name="exchange",
    )(*(pltpu.with_memory_space_constraint(a, pltpu.HBM) for a in arguments))
    return pl.pallas_call(
        functools.partial(store_kernel, len(shapes)),
        out_shape=shapes,
        in_specs=[IN] * 4,
        out_specs=[anywhere] * 4,
        scratch_shapes=[pltpu.SemaphoreType.DMA((len(shapes),))],
        name="store",
    )(*(pltpu.with_memory_space_constraint(a, pltpu.VMEM) for a in held))


MEM = pltpu.VMEM
IN = pl.BlockSpec(memory_space=pltpu.VMEM)


def solution(mesh):
    spread, tracers = P("gy", "gx"), P(None, "gy", "gx")
    return jax.shard_map(
        local,
        mesh=mesh,
        in_specs=(spread, spread, spread, spread, tracers, spread),
        out_specs=(spread, spread, spread, tracers),
        check_vma=False,
    )
```

```python
import functools

import jax
import jax.numpy as jnp
from jax import lax
from jax.experimental import pallas as pl
from jax.experimental.pallas import tpu as pltpu
from jax.sharding import PartitionSpec as P

SUBSTEPS = 3
DIVERGENCE_STEP = 0.3
GRAVITY_STEP = 0.3
DRAG_RATE = 0.05
CORIOLIS_TOP = 0.4
ADVECT_STEP = 0.1

MESH = pl.DeviceIdType.MESH
FIELDS = 7
U, V, LEVEL, MASK, DEPTH, T0, T1 = range(FIELDS)
GROUP = 16
BLOCK = 32
W, E, S, N, SW, SE, NW, NE = range(8)


def roll(x, shift, axis):
    return pltpu.roll(x, shift % x.shape[axis], axis)


def lanes(shape):
    return lax.broadcasted_iota(jnp.int32, shape, 1)


def sublanes(shape):
    return lax.broadcasted_iota(jnp.int32, shape, 0)


def advance(u, v, level, mask, depth, tracers, cor_u, cor_v, row_axis, fold=None):
    col_axis = 1 - row_axis
    west = lambda x: roll(x, 1, col_axis)
    east = lambda x: roll(x, -1, col_axis)
    south = lambda x: roll(x, 1, row_axis)
    north = lambda x: roll(x, -1, row_axis)
    head = lambda x: x[:8]

    def sym(x, other):
        return jnp.concatenate([jnp.where(fold[0], 0.5 * (head(x) - other), head(x)), x[8:]], axis=0)

    east_mask = mask * east(mask)
    north_mask = mask * north(mask)
    depth_u = 0.5 * (depth + east(depth))
    depth_v = 0.5 * (depth + north(depth))
    keep_u = east_mask * (1.0 - DRAG_RATE / depth_u)
    keep_v = north_mask * (1.0 - DRAG_RATE / depth_v)
    push_u = east_mask * (GRAVITY_STEP * depth_u)
    push_v = north_mask * (GRAVITY_STEP * depth_v)
    turn_u = east_mask * (0.25 * cor_u)
    turn_v = north_mask * (0.25 * cor_v)
    spread = DIVERGENCE_STEP * mask
    u = east_mask * u
    v = north_mask * v
    if fold is not None:
        other = head(north_mask) * fold[1]
    for step in range(SUBSTEPS):
        if fold is not None:
            v, other = sym(v, other), 0.5 * (other - head(v))
        flow_west = west(u)
        pair = flow_west + u
        sym_south = south(v)
        level = level - spread * (u - flow_west + v - sym_south)
        both = v + sym_south
        pairs = pair + north(pair)
        slope_v = north(level) - level
        new_u = keep_u * u - push_u * (east(level) - level) + turn_u * (both + east(both))
        if fold is not None:
            other = head(keep_v) * other + head(push_v) * head(slope_v) + head(turn_v) * head(pairs)
        v = keep_v * v - push_v * slope_v - turn_v * pairs
        u = new_u
        sum_u = u if step == 0 else sum_u + u
        sum_v = v if step == 0 else sum_v + v
        if fold is not None:
            sum_other = other if step == 0 else sum_other + other
    mean_u = sum_u * (1.0 / SUBSTEPS)
    mean_v = sum_v * (1.0 / SUBSTEPS)
    if fold is not None:
        mean_v = sym(mean_v, sum_other * (1.0 / SUBSTEPS))
    out_u, in_u = jnp.maximum(mean_u, 0.0), jnp.minimum(mean_u, 0.0)
    out_v, in_v = jnp.maximum(mean_v, 0.0), jnp.minimum(mean_v, 0.0)
    rate = ADVECT_STEP * mask / depth
    new = []
    for t in tracers:
        flux_u = out_u * t + in_u * east(t)
        flux_v = out_v * t + in_v * north(t)
        new.append(t - rate * (flux_u - west(flux_u) + flux_v - south(flux_v)))
    return level, u, v, new[0], new[1]


def pack_last(narrow, wide, x):
    s = sublanes(x[0].shape)
    return [
        jnp.where(s < 1, roll(x[T0], 1, 0), jnp.where(s < 4, roll(x[narrow], 4, 0), x[wide])),
        jnp.where(s < 1, roll(x[T1], 1, 0), jnp.where(s < 4, roll(x[LEVEL], 4, 0), x[MASK])),
        x[DEPTH],
    ]


def pack_first(narrow, wide, x):
    s = sublanes(x[0].shape)
    return [
        jnp.where(s < 3, x[narrow], jnp.where(s < 4, roll(x[T0], 3, 0), roll(x[wide], 4, 0))),
        jnp.where(s < 3, x[LEVEL], jnp.where(s < 4, roll(x[T1], 3, 0), roll(x[MASK], 4, 0))),
        x[DEPTH],
    ]


def unpack_last(narrow, wide, a, b, c):
    x = {narrow: roll(a, 4, 0), wide: a, LEVEL: roll(b, 4, 0), MASK: b, DEPTH: c, T0: roll(a, 7, 0), T1: roll(b, 7, 0)}
    return [x[f] for f in range(FIELDS)]


def unpack_first(narrow, wide, a, b, c):
    x = {narrow: a, wide: roll(a, 4, 0), LEVEL: b, MASK: roll(b, 4, 0), DEPTH: c, T0: roll(a, 5, 0), T1: roll(b, 5, 0)}
    return [x[f] for f in range(FIELDS)]


def put_columns(ref, parts, last):
    a, b, c = parts
    half = c.shape[1] // 2
    left, right = c[:, :half], c[:, half:]
    upper = sublanes(left.shape) < 4
    both = jnp.where(upper, roll(left, 4, 0), right) if last else jnp.where(upper, left, roll(right, 4, 0))
    for k, part in enumerate([a[:, :half], a[:, half:], b[:, :half], b[:, half:], both]):
        ref[8 * k : 8 * k + 8] = part


def get_columns(ref, last):
    both = ref[32:40]
    left, right = (roll(both, 4, 0), both) if last else (both, roll(both, 4, 0))
    pairs = [(ref[0:8], ref[8:16]), (ref[16:24], ref[24:32]), (left, right)]
    return [jnp.concatenate(pair, axis=1) for pair in pairs]


def pack_corner(x, first_row, first_lane):
    row, lane = sublanes(x.shape), lanes(x.shape)
    total = jnp.zeros_like(x)
    for r in range(4):
        here = (row == first_row + r) & (lane & 12 == 4 * r)
        total = total + jnp.where(here, roll(x, 4 * r - first_lane, 1), 0.0)
    return jnp.sum(total, axis=0, keepdims=True)


def unpack_corner(x, first_row, first_lane, base):
    x = jnp.broadcast_to(x, (8, 128))
    row, lane = sublanes(x.shape), lanes(x.shape)
    for r in range(4):
        here = (row == first_row + r) & (lane & 12 == first_lane)
        base = jnp.where(here, roll(x, first_lane - 4 * r, 1), base)
    return base


def flip(x, axis, group):
    at = lax.broadcasted_iota(jnp.int32, x.shape, axis)
    bit = 1
    while bit < group:
        x = jnp.where(at & bit == 0, roll(x, -bit, axis), roll(x, bit, axis))
        bit *= 2
    return x


def exchange_kernel(
    level_in, u_in, v_in, depth_in, tracers_in, land_in,
    level_out, u_out, v_out, tracers_out,
    x, land, packed, packed_t, send_cols, send_rows, send_corners, got_cols, got_rows, got_corners, halo_t, strip, other,
    load_sem, send_sem, recv_sem,
):
    rows, cols = u_out.shape
    nx, ny = lax.axis_size("gx"), lax.axis_size("gy")
    me_x, me_y = lax.axis_index("gx"), lax.axis_index("gy")
    to_e, to_w = lax.rem(me_x + 1, nx), lax.rem(me_x + nx - 1, nx)
    top, bottom = me_y == ny - 1, me_y == 0
    past = lambda column: jnp.where(top, nx - 1 - column, column)
    to_n, to_s = jnp.where(top, me_y, me_y + 1), jnp.where(bottom, me_y, me_y - 1)
    own_ne, own_nw = top & (past(to_e) == me_x), top & (past(to_w) == me_x)
    has_s = jnp.logical_not(bottom)

    barrier = pltpu.get_barrier_semaphore()

    def greet(to_x, to_y):
        pl.semaphore_signal(barrier, inc=1, device_id=(to_x, to_y), device_id_type=MESH)

    greet(to_w, me_y)
    greet(to_e, me_y)
    greet(past(me_x), to_n)
    pl.when(jnp.logical_not(own_ne))(lambda: greet(past(to_e), to_n))
    pl.when(jnp.logical_not(own_nw))(lambda: greet(past(to_w), to_n))

    @pl.when(has_s)
    def _():
        greet(me_x, to_s)
        greet(to_e, to_s)
        greet(to_w, to_s)

    inner = pl.ds(8, rows)
    arguments = [
        (u_in, x.at[U, inner]),
        (v_in, x.at[V, inner]),
        (level_in, x.at[LEVEL, inner]),
        (land_in, land),
        (depth_in, x.at[DEPTH, inner]),
        (tracers_in, x.at[pl.ds(T0, 2), inner]),
    ]

    def load(at, k, columns):
        source, target = arguments[k]
        where = (slice(None),) * (len(source.shape) - 1) + (columns,)
        return pltpu.make_async_copy(source.at[where], target.at[where], load_sem.at[at, k])

    ends = (pl.ds(0, 128), pl.ds(cols - 128, 128))
    end_loads = [[load(at, k, columns) for at, columns in enumerate(ends)] for k in range(len(arguments))]
    middle = pl.ds(128, cols - 256)
    middle_loads = [load(2, k, middle) for k in range(len(arguments))] if cols > 256 else []
    for one in [one for pair in end_loads for one in pair] + middle_loads:
        one.start()
    for f in range(FIELDS):
        x[f, 0:8] = jnp.ones((8, cols), jnp.float32)
        x[f, rows + 8 : rows + 16] = jnp.ones((8, cols), jnp.float32)

    lane = lanes((rows, 128))
    for f in range(FIELDS):
        if f != T1:
            for one in end_loads[f]:
                one.wait()
        if f == MASK:
            first, last = (land[:, columns].astype(jnp.float32) for columns in ends)
        else:
            first, last = (x[f, inner, columns] for columns in ends)
        both = roll(jnp.where(lane < 64, first, last), f * GROUP + 8, 1)
        packed[...] = both if f == 0 else jnp.where(lane < f * GROUP, packed[...], both)
    packed_t[...] = packed[...].T

    groups = [GROUP * f for f in range(FIELDS)]
    north_end, south_end = packed[rows - 8 : rows], packed[0:8]
    send_corners[NE - SW] = pack_corner(north_end, 4, 4)
    send_corners[NW - SW] = pack_corner(north_end, 4, 8)
    send_corners[SE - SW] = pack_corner(south_end, 0, 4)
    send_corners[SW - SW] = pack_corner(south_end, 0, 8)
    put_columns(send_cols.at[0], pack_last(V, U, [packed_t[g : g + 8] for g in groups]), True)
    put_columns(send_cols.at[1], pack_first(V, U, [packed_t[g + 8 : g + 16] for g in groups]), False)

    def copy(source, target, k, at, to_x, to_y):
        return pltpu.make_async_remote_copy(
            src_ref=source,
            dst_ref=target,
            send_sem=send_sem.at[k],
            recv_sem=recv_sem.at[at],
            device_id=(to_x, to_y),
            device_id_type=MESH,
        )

    def corner(k, at, to_x, to_y):
        return copy(send_corners.at[k - SW], got_corners.at[at - SW], k, at, to_x, to_y)

    away_e = copy(send_cols.at[0], got_cols.at[0], E, W, to_e, me_y)
    away_w = copy(send_cols.at[1], got_cols.at[1], W, E, to_w, me_y)
    away_s = copy(send_rows.at[1], got_rows.at[1], S, N, me_x, to_s)
    away_n = copy(send_rows.at[0], got_rows.at[0], N, S, me_x, to_n)
    fold_n = copy(send_rows.at[0], got_rows.at[1], N, N, past(me_x), to_n)
    away_se, away_sw = corner(SE, NW, to_e, to_s), corner(SW, NE, to_w, to_s)
    away_ne, away_nw = corner(NE, SW, to_e, to_n), corner(NW, SE, to_w, to_n)
    fold_ne, fold_nw = corner(NE, NE, past(to_e), to_n), corner(NW, NW, past(to_w), to_n)
    not_top = jnp.logical_not(top)
    far_ne, far_nw = top & jnp.logical_not(own_ne), top & jnp.logical_not(own_nw)

    count = 3 + jnp.where(own_ne, 0, 1) + jnp.where(own_nw, 0, 1) + jnp.where(has_s, 3, 0)
    def send_far():
        pl.when(not_top)(lambda: away_ne.start())
        pl.when(far_ne)(lambda: fold_ne.start())
        pl.when(has_s)(lambda: away_se.start())
        away_e.start()
        pl.when(not_top)(lambda: away_nw.start())
        pl.when(far_nw)(lambda: fold_nw.start())
        pl.when(has_s)(lambda: away_sw.start())
        away_w.start()

    def send_near():
        pl.when(not_top)(lambda: away_n.start())
        pl.when(top)(lambda: fold_n.start())
        pl.when(has_s)(lambda: away_s.start())

    odd = lax.rem(me_x, 2)

    @pl.when(odd == 1)
    def _():
        pl.semaphore_wait(barrier, count)
        send_far()

    for one in middle_loads:
        one.wait()
    x[MASK, inner] = land[...].astype(jnp.float32)
    send_rows[0] = jnp.concatenate(pack_last(U, V, [x[f, rows : rows + 8] for f in range(FIELDS)]), axis=0)
    send_rows[1] = jnp.concatenate(pack_first(U, V, [x[f, 8:16] for f in range(FIELDS)]), axis=0)
    pl.when(odd == 1)(send_near)

    def coriolis(row):
        row = row.astype(jnp.float32)
        total = 1.0 * ny * rows
        return CORIOLIS_TOP * ((row + 0.5) / total), CORIOLIS_TOP * ((row + 1.0) / total)

    def compute_inner(k, carry):
        at = pl.multiple_of(k * BLOCK, BLOCK)
        part = [x[f, pl.ds(at, BLOCK + 16)] for f in range(FIELDS)]
        row = me_y * rows + at - 8 + sublanes((BLOCK + 16, 1))
        out = advance(*part[:5], part[5:], *coriolis(row), 0)
        keep = pl.ds(at, BLOCK)
        level_out[keep] = out[0][8 : BLOCK + 8]
        u_out[keep] = out[1][8 : BLOCK + 8]
        v_out[keep] = out[2][8 : BLOCK + 8]
        tracers_out[0, keep] = out[3][8 : BLOCK + 8]
        tracers_out[1, keep] = out[4][8 : BLOCK + 8]
        return carry

    blocks = rows // BLOCK
    lax.fori_loop(0, blocks * (1 - odd), compute_inner, 0)

    @pl.when(odd == 0)
    def _():
        pl.semaphore_wait(barrier, count)
        send_near()
        send_far()

    lax.fori_loop(blocks * (1 - odd), blocks, compute_inner, 0)

    away_w.wait_recv()
    away_e.wait_recv()
    away_s.wait_recv()

    @pl.when(has_s)
    def _():
        away_n.wait_recv()
        away_ne.wait_recv()
        away_nw.wait_recv()

    pl.when(jnp.logical_not(own_nw))(lambda: away_se.wait_recv())
    pl.when(jnp.logical_not(own_ne))(lambda: away_sw.wait_recv())

    @pl.when(own_nw)
    def _():
        got_corners[NW - SW] = send_corners[NW - SW]

    @pl.when(own_ne)
    def _():
        got_corners[NE - SW] = send_corners[NE - SW]

    from_w = unpack_last(V, U, *get_columns(got_cols.at[0], True))
    from_e = unpack_first(V, U, *get_columns(got_cols.at[1], False))
    for f, g in enumerate(groups):
        halo_t[g : g + 8] = from_w[f]
        halo_t[g + 8 : g + 16] = from_e[f]
    halo_t[GROUP * FIELDS :] = jnp.ones((128 - GROUP * FIELDS, rows), jnp.float32)

    def put_rows(at, parts, sides):
        for f in range(FIELDS):
            strip[f, at : at + 8, 0:cols] = parts[f]
            strip[f, at : at + 8, cols : cols + 128] = roll(sides, -(GROUP * f + 8), 1)

    put_rows(0, [x[f, rows : rows + 8] for f in range(FIELDS)], halo_t[:, rows - 128 : rows].T[120:128])
    put_rows(24, [x[f, 8:16] for f in range(FIELDS)], halo_t[:, 0:128].T[0:8])
    from_n, from_s = ([ref[0:8], ref[8:16], ref[16:24]] for ref in (got_rows.at[1], got_rows.at[0]))
    from_ne, from_nw, from_se, from_sw = (got_corners[k - SW] for k in (NE, NW, SE, SW))
    nothing = jnp.zeros((8, 128), jnp.float32)

    sides = unpack_corner(from_ne, 0, 8, unpack_corner(from_nw, 0, 4, nothing))
    put_rows(8, unpack_first(U, V, *from_n), sides)
    other[...] = jnp.zeros_like(other)
    sides = unpack_corner(from_se, 4, 8, unpack_corner(from_sw, 4, 4, nothing))
    put_rows(16, unpack_last(U, V, *from_s), sides)

    @pl.when(top)
    def _():
        parts = [flip(part, 0, 8) for part in unpack_last(U, V, *from_n)]
        tiles = range(0, cols, 128)
        parts = [
            jnp.concatenate([flip(part[:, c : c + 128], 1, 128) for c in reversed(tiles)], axis=1)
            for part in parts
        ]
        sides = unpack_corner(flip(from_nw, 1, GROUP), 0, 4, nothing)
        put_rows(8, parts, unpack_corner(flip(from_ne, 1, GROUP), 0, 8, sides))
        strip[U, 8:16] = -roll(strip[U, 8:16], -1, 1)
        mirrored = strip[V, 8:16]
        strip[V, 8:16] = -roll(mirrored, -1, 0)
        other[...] = roll(mirrored, -1, 0)

    @pl.when(bottom)
    def _():
        for f in range(FIELDS):
            strip[f, 16:24] = jnp.full((8, cols + 128), 1.0 if f == DEPTH else 0.0, jnp.float32)

    upper = sublanes((8, rows)) < 4
    parts = [
        jnp.concatenate(
            [packed_t[g : g + 8], jnp.where(upper, halo_t[g + 8 : g + 16], halo_t[g : g + 8]), packed_t[g + 8 : g + 16]],
            axis=0,
        )
        for g in groups
    ]
    row = me_y * rows + lanes((1, rows))
    by_col = advance(*parts[:5], parts[5:], *coriolis(row), 1)

    s = sublanes((24, 1))
    row = me_y * rows + jnp.where(s < 12, rows - 8 + s, s - 16)
    total = ny * rows
    cor_u = coriolis(jnp.where(row >= total, 2 * total - 1 - row, row))[0]
    cor_v = coriolis(jnp.where(row >= total, 2 * total - 2 - row, row))[1]
    upper = sublanes((8, cols + 128)) < 4
    parts = [
        jnp.concatenate([strip[f, 0:8], jnp.where(upper, strip[f, 8:16], strip[f, 16:24]), strip[f, 24:32]], axis=0)
        for f in range(FIELDS)
    ]
    at_fold = top & (sublanes((8, cols + 128)) == 7)
    by_row = advance(*parts[:5], parts[5:], cor_u, cor_v, 0, (at_fold, other[...]))

    zeros = jnp.zeros((128 - GROUP * 5, rows), jnp.float32)
    back = jnp.concatenate([part for o in by_col for part in (o[0:8], o[16:24])] + [zeros], axis=0).T
    outs = [level_out, u_out, v_out, tracers_out.at[0], tracers_out.at[1]]
    lane = lanes((rows, 128))
    s = sublanes((8, cols))
    for o, out in enumerate(outs):
        ends = roll(back, -(GROUP * o + 8), 1)
        out[:, 0:128] = jnp.where(lane < 4, ends, out[:, 0:128])
        out[:, cols - 128 : cols] = jnp.where(lane >= 124, ends, out[:, cols - 128 : cols])
        out[0:8] = jnp.where(s < 4, by_row[o][16:24, 0:cols], out[0:8])
        out[rows - 8 : rows] = jnp.where(s >= 4, by_row[o][0:8, 0:cols], out[rows - 8 : rows])

    away_e.wait_send()
    away_w.wait_send()

    @pl.when(not_top)
    def _():
        away_ne.wait_send()
        away_nw.wait_send()
        away_n.wait_send()

    @pl.when(top)
    def _():
        fold_n.wait_send()

    pl.when(far_ne)(lambda: fold_ne.wait_send())
    pl.when(far_nw)(lambda: fold_nw.wait_send())

    @pl.when(has_s)
    def _():
        away_se.wait_send()
        away_sw.wait_send()
        away_s.wait_send()


def store_kernel(count, *refs):
    sems = refs[-1]
    copies = [pltpu.make_async_copy(refs[k], refs[count + k], sems.at[k]) for k in reversed(range(count))]
    for one in copies:
        one.start()
    for one in copies:
        one.wait()


def local(*arguments):
    rows, cols = arguments[0].shape
    f32 = jnp.float32
    plane, pair = jax.ShapeDtypeStruct((rows, cols), f32), jax.ShapeDtypeStruct((2, rows, cols), f32)
    shapes = [plane, plane, plane, pair]
    anywhere, vmem = pl.BlockSpec(memory_space=pl.ANY), pl.BlockSpec(memory_space=pltpu.VMEM)
    held = pl.pallas_call(
        exchange_kernel,
        out_shape=[MEM(s.shape, s.dtype) for s in shapes],
        in_specs=[anywhere] * 6,
        out_specs=[vmem] * 4,
        scratch_shapes=[
            pltpu.VMEM((FIELDS, rows + 16, cols), f32),
            pltpu.VMEM((rows, cols), jnp.int32),
            pltpu.VMEM((rows, 128), f32),
            pltpu.VMEM((128, rows), f32),
            pltpu.VMEM((2, 40, rows // 2), f32),
            pltpu.VMEM((2, 24, cols), f32),
            pltpu.VMEM((4, 1, 128), f32),
            pltpu.VMEM((2, 40, rows // 2), f32),
            pltpu.VMEM((2, 24, cols), f32),
            pltpu.VMEM((4, 1, 128), f32),
            pltpu.VMEM((128, rows), f32),
            pltpu.VMEM((FIELDS, 32, cols + 128), f32),
            pltpu.VMEM((8, cols + 128), f32),
            pltpu.SemaphoreType.DMA((3, 6)),
            pltpu.SemaphoreType.DMA((8,)),
            pltpu.SemaphoreType.DMA((8,)),
        ],
        compiler_params=pltpu.CompilerParams(collective_id=0, has_side_effects=True, vmem_limit_bytes=32 * 2**20),
        name="exchange",
    )(*(pltpu.with_memory_space_constraint(a, pltpu.HBM) for a in arguments))
    return pl.pallas_call(
        functools.partial(store_kernel, len(shapes)),
        out_shape=shapes,
        in_specs=[IN] * 4,
        out_specs=[anywhere] * 4,
        scratch_shapes=[pltpu.SemaphoreType.DMA((len(shapes),))],
        name="store",
    )(*(pltpu.with_memory_space_constraint(a, pltpu.VMEM) for a in held))


MEM = pltpu.VMEM
IN = pl.BlockSpec(memory_space=pltpu.VMEM)


def solution(mesh):
    spread, tracers = P("gy", "gx"), P(None, "gy", "gx")
    return jax.shard_map(
        local,
        mesh=mesh,
        in_specs=(spread, spread, spread, spread, tracers, spread),
        out_specs=(spread, spread, spread, tracers),
        check_vma=False,
    )
```
